32 devices in a mesh: groups: 2 (over x), row: 8 (over z, y), col: 2 (over core).
Axes of the slice: x: 2, y: 2, z: 4, core: 2. Of those that a mesh axis runs over, the one named last changes fastest.
Arguments:
- vectors: bfloat16 [131072, 32], P(('groups', 'row')), parts along dimension 0, may hold values from -6 to 6
- coords: bfloat16 [3, 65536], P(None, 'row'), may hold values from 0 to 1
- sigma: bfloat16 [131072], P(('groups', 'row')), parts along dimension 0, may hold values from 0.079589844 to 0.796875
- counts: int32 [256], replicated, may hold values from 1 to 24, as said below
- columns: int32 [256, 24], replicated, may hold values from 0 to 255, as said below
Outputs:
- product_field: float32 [131072, 32], P(('groups', 'row', 'col')), parts along dimension 0
The draws below stay inside these ranges and needn't reach their ends.
There are 2 independent parts, one for each index of `groups`. The reference program is written for one: setup_inputs(seed, part) draws one part's arguments, and reference() takes and returns one part's arrays. A program takes and returns all parts, laid end to end along the dimension named above; an argument that names none is the same for every part. Nothing has to cross between parts.
Inputs may be any that keep to these rules, and one draw needn't show every extreme that they name: counts[i] is at most min(24, 256 - i); block row 0 has exactly 24. `columns`: in block row i the first counts[i] entries are distinct, the first is i and the others lie between i + 1 and min(i + 96, 256) - 1; the entries past them equal i.
All inputs are finite; a program needn't handle non-finite values.
Results may differ from the reference program's by a relative error of at most 0.0029.
Values may be sent and summed in bfloat16 or wider, within the bound.
No kernel may reach another device: no remote copies, remote signals or barrier semaphores. Data moves between devices by JAX's collectives and lax.ppermute only.
A program may use at most 64 MiB of HBM per device.

```python
import math
import jax
import jax.numpy as jnp
from jax import lax

BLK = 256
NV = 32
KMAX = 24
WIN = 96
NB = 256
NCELL = 65536


def pattern_draw(key):
    first_key, second_key = jax.random.split(key)
    rows_all = jnp.arange(NB, dtype=jnp.int32)
    wanted = jax.random.randint(first_key, (NB,), KMAX // 4, KMAX + 1, dtype=jnp.int32)
    wanted = wanted.at[0].set(KMAX)
    room = jnp.minimum(WIN, NB - rows_all)
    degree = jnp.minimum(wanted, room).astype(jnp.int32)
    offsets = jnp.arange(1, WIN, dtype=jnp.int32)
    scores = jax.random.randint(second_key, (NB, WIN - 1), 0, 1 << 20, dtype=jnp.int32) * WIN + offsets[None, :]
    inside = rows_all[:, None] + offsets[None, :] < NB
    scores = jnp.where(inside, scores, -offsets[None, :])
    top_scores, chosen = lax.top_k(scores, KMAX - 1)
    further = rows_all[:, None] + 1 + chosen.astype(jnp.int32)
    full_list = jnp.concatenate([rows_all[:, None], further], axis=1)
    slot_ids = jnp.arange(KMAX, dtype=jnp.int32)
    full_list = jnp.where(slot_ids[None, :] < degree[:, None], full_list, rows_all[:, None])
    return (full_list.astype(jnp.int32), degree)


def draw_counts(key, part):
    return pattern_draw(key)[1]


def draw_columns(key, part):
    return pattern_draw(key)[0]


def draw_coords(key, part):
    key = jax.random.fold_in(key, 7)
    period = 5 * WIN
    block_ids = jnp.arange(NB, dtype=jnp.int32)
    pass_ids = block_ids // period
    step_ids = block_ids % period
    frac = step_ids.astype(jnp.float32) / period
    forward = pass_ids % 2 == 0
    along = jnp.where(forward, frac, 1.0 - frac)
    centre_x = 0.06 + 0.88 * along
    centre_y = 0.1 + 0.15 * (pass_ids % 6).astype(jnp.float32)
    centre_z = jnp.full((NB,), 0.5, jnp.float32)
    centres = jnp.stack([centre_x, centre_y, centre_z], axis=0)
    jitter = jax.random.uniform(key, (3, NB, BLK), jnp.float32, -0.06, 0.06)
    cells = centres[:, :, None] + jitter
    cells = jnp.clip(cells, 0.0, 1.0)
    return cells.reshape(3, NB * BLK).astype(jnp.bfloat16)


def level_of(stream_key, extent, pieces, least, top_value):
    loudness, own = 1.0, jax.random.fold_in(stream_key, 6)
    for position, blocks in pieces:
        steps = jnp.exp(jax.random.uniform(jax.random.fold_in(own, position), (blocks,), jnp.float32, least / len(pieces), top_value / len(pieces)))
        loudness = loudness * jnp.repeat(steps, extent[position] // blocks).reshape([-1 if axis == position else 1 for axis in range(len(extent))])
    return loudness


def normal_values(rng, dims, width, limit, pieces=(), held_as=jnp.bfloat16):
    factor_of = level_of(rng, dims, pieces, -0.22, 0.18) if pieces else 1.0
    array = jax.random.normal(rng, dims, jnp.float32) * width * factor_of
    return jnp.minimum(jnp.maximum(array, -limit), limit).astype(held_as)


def setup_inputs(seed: int = 0, part: int = 0) -> dict:
    key_of = jax.random.split(jax.random.key(seed), 6)
    part_splits = jax.random.split(jax.random.fold_in(key_of[5], part), 6)
    vectors = normal_values(part_splits[0], (NCELL, NV), 1.0, 6.0, ((0, 8),))
    coords = draw_coords(jax.random.fold_in(key_of[5], 71), part)
    sigma = jnp.clip(jnp.exp(math.log(0.796875) - 2.3038113 * jax.random.uniform(part_splits[2], (NCELL,), jnp.float32) ** level_of(part_splits[2], (NCELL,), ((0, 8),), -0.2, 0.2)), 0.079589844, 0.796875).astype(jnp.bfloat16)
    counts = draw_counts(jax.random.fold_in(key_of[5], 71), part)
    columns = draw_columns(jax.random.fold_in(key_of[5], 71), part)
    return {"vectors": vectors, "coords": coords, "sigma": sigma, "counts": counts, "columns": columns}


corr_length = 0.12
support_radius = 0.3
nugget_share = 1.0
sqrt_three = math.sqrt(3.0)

def kernel_block(points_row, spread_row, points_col, spread_col, diagonal_flag):
    size_row = points_row.shape[2]
    size_col = points_col.shape[2]
    squared = jnp.zeros((points_row.shape[0], size_row, size_col), jnp.float32)
    for component in range(3):
        offset = points_row[:, component, :, None] - points_col[:, component, None, :]
        squared = squared + offset * offset
    distance = jnp.sqrt(squared)
    scaled = sqrt_three * distance / corr_length
    matern = (1.0 + scaled) * jnp.exp(-scaled)
    ratio = distance / support_radius
    taper = jnp.maximum(1.0 - ratio, 0.0) ** 4 * (1.0 + 4.0 * ratio)
    values = spread_row[:, :, None] * spread_col[:, None, :] * matern * taper
    identity = (lax.broadcasted_iota(jnp.int32, (size_row, size_col), 0) == lax.broadcasted_iota(jnp.int32, (size_row, size_col), 1)).astype(jnp.float32)
    weight = jnp.where(diagonal_flag, nugget_share, 0.0)
    extra = weight[:, None, None] * identity[None] * (spread_row * spread_row)[:, :, None]
    return (values + extra).astype(jnp.bfloat16)

def reference(vectors, coords, sigma, counts, columns):
    block_count = counts.shape[0]
    blocks = vectors.reshape(block_count, BLK, NV).astype(jnp.float32)
    points = coords.astype(jnp.float32).reshape(3, block_count, BLK).transpose(1, 0, 2)
    spreads = sigma.astype(jnp.float32).reshape(block_count, BLK)
    slot_ids = jnp.arange(KMAX, dtype=jnp.int32)

    def one_row(totals, block_row):
        targets = columns[block_row]
        active = (slot_ids < counts[block_row]).astype(jnp.float32)
        row_points = jnp.broadcast_to(points[block_row][None], (KMAX, 3, BLK))
        row_spread = jnp.broadcast_to(spreads[block_row][None], (KMAX, BLK))
        tile_block = kernel_block(row_points, row_spread, points[targets], spreads[targets], targets == block_row).astype(jnp.float32)
        toward_row = jnp.einsum('kab,kbv->av', tile_block * active[:, None, None], blocks[targets])
        mirror = active * (targets != block_row).astype(jnp.float32)
        toward_cols = jnp.einsum('kab,av->kbv', tile_block, blocks[block_row]) * mirror[:, None, None]
        totals = totals.at[block_row].add(toward_row).at[targets].add(toward_cols)
        return (totals, None)
    totals, unused = lax.scan(one_row, jnp.zeros((block_count, BLK, NV), jnp.float32), jnp.arange(block_count, dtype=jnp.int32))
    return totals.reshape(block_count * BLK, NV)
```

```python
import functools
import math

import jax
import jax.numpy as jnp
from jax import lax
from jax.experimental import pallas as pl
from jax.experimental.pallas import tpu as pltpu
from jax.sharding import PartitionSpec as P

BLK = 256
NV = 32
KMAX = 24
FEAT = 16
REACH = 3
PIECES = 8
FILL = 64
CHUNK = 32

CORR = 0.12
SUPPORT = 0.3
SCALE = math.sqrt(3.0) / CORR * math.log2(math.e)
EDGE = SUPPORT * SCALE
SHIFT_U = 1.0 / math.log(2.0)
SHIFT_T = EDGE / 4.0
FACTOR = math.log(2.0) * 4.0 / EDGE**5 * 2.0**-EDGE


def split3(x):
    high = x.astype(jnp.bfloat16).astype(jnp.float32)
    rest = x - high
    mid = rest.astype(jnp.bfloat16).astype(jnp.float32)
    low = (rest - mid).astype(jnp.bfloat16).astype(jnp.float32)
    return [high, mid, low]


def message_kernel(vectors, coords_any, sigma_any, part, coords, sigma, rows, sems):
    half = vectors.shape[1] // 2
    core = lax.axis_index("col")
    begin = pl.multiple_of(core * half, half)
    copies = [
        pltpu.make_async_copy(coords_any, coords, sems.at[0]),
        pltpu.make_async_copy(sigma_any, sigma, sems.at[1]),
        pltpu.make_async_copy(vectors.at[:, pl.ds(begin, half)], part.at[:, pl.ds(0, half)], sems.at[2]),
    ]
    for copy in copies:
        copy.start()
    copies[0].wait()
    width = half // PIECES
    mine = coords[:, pl.ds(begin, half)].astype(jnp.float32)
    for axis in range(3):
        for piece in range(PIECES):
            rows[axis * PIECES + piece : axis * PIECES + piece + 1, :] = mine[
                axis : axis + 1, piece * width : (piece + 1) * width
            ]
    copies[1].wait()
    count = half // 128
    spread = sigma[pl.ds(pl.multiple_of(core * count, count), count), :].astype(jnp.float32)
    for row in range(count):
        piece, place = divmod(row * 128, width)
        rows[3 * PIECES + piece : 3 * PIECES + piece + 1, place : place + 128] = spread[row : row + 1, :]
    part[:, half:] = rows[...].astype(jnp.bfloat16)
    copies[2].wait()


def column_factors(points, spread, b_rows):
    norms = split3(SCALE * SCALE * (points[0:1] * points[0:1] + points[1:2] * points[1:2] + points[2:3] * points[2:3]))
    for index in range(3):
        b_rows[3 * index : 3 * index + 3, :] = points
        b_rows[9 + index : 10 + index, :] = norms[index]
    b_rows[12:15, :] = jnp.ones_like(points)
    if spread is not None:
        b_rows[15:16, :] = spread
    return norms


def unpack(message, rows, b_rows, b, w):
    half = b.shape[1]
    width = half // PIECES
    packed = message[:, half:].astype(jnp.float32)
    for row in range(4 * PIECES):
        index, piece = divmod(row, PIECES)
        rows[index : index + 1, piece * width : (piece + 1) * width] = packed[row : row + 1, :]
    column_factors(rows[0:3, :], rows[3:4, :], b_rows)
    b[...] = b_rows[...].astype(jnp.bfloat16)
    scaled(message[:, :half], rows[3:4, :], w)


def scaled(vectors, spread, out):
    product = vectors.astype(jnp.float32) * spread
    high = product.astype(jnp.bfloat16)
    out[0:NV, :] = high
    out[NV:, :] = (product - high.astype(jnp.float32)).astype(jnp.bfloat16)


def prepare_kernel(rows_dev, counts, columns, coords, sigma, vectors, out, a_out, b_out, w_out, b_rows, a_rows):
    points = coords[...].astype(jnp.float32)
    norms = column_factors(points, None, b_rows)
    cross = split3(-2.0 * SCALE * SCALE * points)
    a_rows[...] = jnp.zeros_like(a_rows)
    a_rows[9:12, :] = jnp.ones_like(points)
    for index in range(3):
        a_rows[3 * index : 3 * index + 3, :] = cross[index]
        a_rows[12 + index : 13 + index, :] = norms[index]
    spread = sigma[...].astype(jnp.float32)
    for row in range(sigma.shape[0]):
        piece = spread[row : row + 1, :]
        b_rows[15:16, row * 128 : (row + 1) * 128] = piece
    b_out[...] = b_rows[...].astype(jnp.bfloat16)
    scaled(vectors[...], b_rows[15:16, :], w_out)
    for block in range(rows_dev):
        cells = slice(block * BLK, (block + 1) * BLK)
        a_out[cells, :] = a_rows[:, cells].T.astype(jnp.bfloat16)
    half = rows_dev // 2
    core = lax.axis_index("col")
    total = rows_dev * KMAX
    first_row = lax.axis_index("row") * rows_dev
    window = columns[:, pl.ds(pl.multiple_of((first_row >> 7) * 128, 128), 128)]
    window = pltpu.roll(window, (128 - (first_row & 127)) & 127, 1)
    window = jnp.concatenate([window, jnp.zeros((128 - KMAX, 128), jnp.int32)], axis=0)
    ahead = window.astype(jnp.float32).T[0:rows_dev].astype(jnp.int32) - first_row
    row = lax.broadcasted_iota(jnp.int32, ahead.shape, 0)
    slot = lax.broadcasted_iota(jnp.int32, ahead.shape, 1)
    live_slots = jnp.zeros(ahead.shape, jnp.int32)
    for index in range(rows_dev):
        live_slots = jnp.where(row == index, counts[first_row + index], live_slots)
    step = ahead >> 5
    col = ahead & 31
    live = (slot < live_slots) & (ahead != row)
    local = step == 0
    same_half = (row >> 4) == (col >> 4)
    mine = (col >> 4) == core
    phase = jnp.where(local, jnp.where(same_half, 4, 0), step)
    phase = jnp.where(mine | (phase == 0), phase, 5)
    phase = jnp.where(live, phase, 6)
    phase = jnp.where(slot < KMAX, phase, 99)
    code = row * 64 + jnp.where(local, col, col & (half - 1))
    stack = jnp.concatenate([(phase == index).astype(jnp.float32) for index in range(8)], axis=0).astype(jnp.bfloat16)
    size = stack.shape[0]
    width = ahead.shape[1]

    def order(shape, first, second):
        return (
            lax.broadcasted_iota(jnp.int32, shape, first) < lax.broadcasted_iota(jnp.int32, shape, second)
        ).astype(jnp.float32).astype(jnp.bfloat16)

    in_row = jnp.dot(stack, order((width, width), 0, 1), preferred_element_type=jnp.float32)
    row_sum = jnp.dot(stack, jnp.ones((width, width), jnp.bfloat16), preferred_element_type=jnp.float32)
    above = jnp.dot(order((size, size), 1, 0), row_sum.astype(jnp.bfloat16), preferred_element_type=jnp.float32)
    rank = jnp.full(ahead.shape, -1.0, jnp.float32)
    for index in range(8):
        rows = slice(index * rows_dev, (index + 1) * rows_dev)
        rank = jnp.where(phase == index, in_row[rows] + above[rows], rank)
    rank = rank.astype(jnp.int32)
    place = lax.broadcasted_iota(jnp.int32, (rows_dev, total), 1)
    codes = code.astype(jnp.float32)
    picked = jnp.zeros((rows_dev, total), jnp.float32)
    for index in range(KMAX):
        picked = picked + jnp.where(rank[:, index : index + 1] == place, codes[:, index : index + 1], 0.0)
    out[0:1, 0:total] = jnp.sum(picked, axis=0, keepdims=True).astype(jnp.int32)
    chosen = lax.broadcasted_iota(jnp.int32, above.shape, 0) == rows_dev * lax.broadcasted_iota(jnp.int32, above.shape, 1)
    out[0:1, total : total + width] = jnp.sum(jnp.where(chosen, above, 0.0), axis=0, keepdims=True).astype(jnp.int32)


def phase_run(meta, rows_dev, phase):
    base = rows_dev * KMAX
    first = meta[0, base + phase]
    size = meta[0, base + phase + 1] - first
    if phase == 0:
        mine = meta[0, base + 5] - meta[0, base + 1]
        other = meta[0, base + 6] - meta[0, base + 5]
        core = lax.axis_index("col")
        load0 = jnp.where(core == 0, mine, other)
        load1 = jnp.where(core == 0, other, mine)
        lead = jnp.clip((load1 - load0 + size) >> 1, 0, size)
        first = jnp.where(core == 0, 0, lead)
        size = jnp.where(core == 0, lead, size - lead)
    return first, size


def lanes(index):
    return pl.ds(pl.multiple_of(index * BLK, BLK), BLK)


def fill_tile(dist, tile, slot):
    for chunk in range(BLK // CHUNK):
        rows = pl.ds(chunk * CHUNK, CHUNK)
        square = jnp.maximum(dist[slot, rows], 1e-12)
        rho = square * lax.rsqrt(square)
        inner = jnp.maximum(EDGE - rho, 0.0)
        inner2 = inner * inner
        shape = (inner2 * inner2) * ((rho + SHIFT_U) * (rho + SHIFT_T)) * jnp.exp2(inner)
        tile[slot, rows] = shape.astype(jnp.bfloat16)


def sweep(size, entry, a_ref, row_ref, col_ref, b_ref, dist, tile, add_row, add_col):
    def distances(step, slot):
        i, j = entry(step)
        dist[slot] = jnp.dot(a_ref[lanes(i), :], b_ref[:, lanes(j)], preferred_element_type=jnp.float32)

    @pl.when(size > 0)
    def _():
        distances(0, 0)

    def two_steps(turn, carry):
        additions = []
        for slot in range(2):
            step = turn * 2 + slot
            i, j = entry(step - 1)
            live = (step >= 1) & (step <= size)
            block = tile[1 - slot]
            toward_row = lax.dot_general(
                col_ref[:, lanes(j)], block, (((1,), (1,)), ((), ())), preferred_element_type=jnp.float32
            )
            additions.append((add_row, i, live, toward_row))
            if add_col is not None:
                toward_col = jnp.dot(row_ref[:, lanes(i)], block, preferred_element_type=jnp.float32)
                additions.append((add_col, j, live, toward_col))
            fill_tile(dist, tile, slot)
            distances(step + 1, 1 - slot)
        for add, block, live, value in additions:
            add(block, live, value[:NV] + value[NV:])
        return carry

    lax.fori_loop(0, jnp.where(size > 0, (size + 2) // 2, 0), two_steps, 0)


def adder(acc, spare, index):
    def add(block, live, value):
        where = lanes(jnp.where(live, index(block), spare))
        acc[:, where] = acc[:, where] + value

    return add


def listed(meta, start, size):
    def entry(step):
        code = meta[0, start + jnp.clip(step, 0, jnp.maximum(size - 1, 0))]
        return code >> 6, code & 63

    return size, entry


def diagonal_blocks(rows_dev, core):
    half = rows_dev // 2

    def entry(step):
        block = core * half + jnp.clip(step, 0, half - 1)
        return block, block

    return entry


def near_kernel(rows_dev, meta, a_ref, w_ref, b_ref, acc, dist, tile):
    half = rows_dev // 2
    core = lax.axis_index("col")
    acc[...] = jnp.zeros_like(acc)
    add = adder(acc, rows_dev, lambda block: block ^ (core * half))
    sweep(half, diagonal_blocks(rows_dev, core), a_ref, w_ref, w_ref, b_ref, dist, tile, add, None)


def ahead_kernel(phase, rows_dev, meta, a_ref, w_ref, message, before, *refs):
    half = rows_dev // 2
    core = lax.axis_index("col")
    if phase == 1:
        kept, given, back, dist, tile, acc_col, rows, b_rows, b, w, acc = refs
    elif phase == 3:
        b_ref, back2, acc, back, dist, tile, acc_col, rows, b_rows, b, w = refs
    else:
        b_ref, acc, back, dist, tile, acc_col, rows, b_rows, b, w = refs
    acc[...] = before[...]
    acc_col[...] = jnp.zeros_like(acc_col)
    if phase == 2:
        unpack(message, rows, b_rows, b, w)
    else:
        unpack(message.at[pl.ds(0 if phase == 1 else NV, NV)], rows, b_rows, b, w)
    add_row = adder(acc, rows_dev, lambda block: block ^ (core * half))
    add_col = adder(acc_col, half, lambda block: block)
    size, entry = listed(meta, *phase_run(meta, rows_dev, phase))
    sweep(size, entry, a_ref, w_ref, w, b, dist, tile, add_row, add_col)
    if phase != 1:
        start, size = phase_run(meta, rows_dev, 0)
        early = jnp.clip(FILL - phase_run(meta, rows_dev, 2)[1], 0, size)
        if phase == 2:
            size = early
        else:
            start, size = start + early, size - early
        size, entry = listed(meta, start, size)
        sweep(size, entry, a_ref, w_ref, w_ref, b_ref, dist, tile, add_row, add_row)
    sums = acc_col[:, : half * BLK].astype(back.dtype)
    if phase == 3:
        back[0:NV, :] = back2[...]
        back[NV:, :] = sums
    else:
        back[...] = sums
    if phase == 1:
        kept[...] = acc[:, : half * BLK]
        given[...] = acc[:, half * BLK : 2 * half * BLK]


def join_kernel(own, got, out):
    out[0:NV, :] = own[...]
    out[NV:, :] = got[...]


def onward_kernel(back, got, out):
    out[...] = (back[...] + got[NV:, :].astype(jnp.float32)).astype(out.dtype)


def inside_kernel(rows_dev, meta, a_ref, w_ref, b_ref, kept, got, vectors, out, scale, dist, tile, acc):
    half = rows_dev // 2
    acc[:, : half * BLK] = kept[...] + got[0:NV, :].astype(jnp.float32)
    acc[:, half * BLK :] = jnp.zeros((NV, BLK), jnp.float32)
    add = adder(acc, half, lambda block: block & (half - 1))
    size, entry = listed(meta, *phase_run(meta, rows_dev, 4))
    sweep(size, entry, a_ref, w_ref, w_ref, b_ref, dist, tile, add, add)
    width = half * BLK
    mine = pl.ds(pl.multiple_of(lax.axis_index("col") * width, width), width)
    spread = b_ref[:, mine].astype(jnp.float32)[FEAT - 1 : FEAT, :]
    scale[...] = FACTOR * spread
    out[...] = acc[:, :width] * (FACTOR * spread) + spread * spread * vectors[:, mine].astype(jnp.float32)


def estimate(microseconds):
    return pl.CostEstimate(flops=int(microseconds * 1.15e9), bytes_accessed=1 << 20, transcendentals=0)


def run(kernel, name, tiles, out_shape, scratch, operands):
    smem = pl.BlockSpec(memory_space=pltpu.SMEM)
    vmem = pl.BlockSpec(memory_space=pltpu.VMEM)
    multiple = isinstance(out_shape, tuple)
    return pl.pallas_call(
        kernel,
        out_shape=out_shape,
        in_specs=[smem] + [vmem] * (len(operands) - 1),
        out_specs=tuple(vmem for _ in out_shape) if multiple else vmem,
        scratch_shapes=[
            pltpu.VMEM((2, BLK, BLK), jnp.float32),
            pltpu.VMEM((2, BLK, BLK), jnp.bfloat16),
        ]
        + scratch,
        compiler_params=pltpu.CompilerParams(vmem_limit_bytes=28 * 1024 * 1024),
        cost_estimate=estimate(0.17 * tiles),
        name=name,
    )(*operands)


def local(vectors, coords, sigma, counts, columns):
    cells = vectors.shape[0]
    rows_dev = cells // BLK
    half_cells = cells // 2
    row_devices = lax.axis_size("row")
    smem = pl.BlockSpec(memory_space=pltpu.SMEM)
    vmem = pl.BlockSpec(memory_space=pltpu.VMEM)
    own = vectors.T
    sigma = sigma.reshape(cells // 128, 128)

    part = pl.pallas_call(
        message_kernel,
        out_shape=jax.ShapeDtypeStruct((NV, half_cells + half_cells // PIECES), jnp.bfloat16),
        in_specs=[pl.BlockSpec(memory_space=pltpu.HBM)] * 3,
        out_specs=vmem,
        scratch_shapes=[
            pltpu.VMEM(coords.shape, jnp.bfloat16),
            pltpu.VMEM(sigma.shape, jnp.bfloat16),
            pltpu.VMEM((4 * PIECES, half_cells // PIECES), jnp.float32),
            pltpu.SemaphoreType.DMA((3,)),
        ],
        compiler_params=pltpu.CompilerParams(vmem_limit_bytes=60 * 1024 * 1024),
        cost_estimate=estimate(2.0),
        name="message",
    )(own, coords, sigma)

    def from_ahead(block, stride):
        return lax.ppermute(block, "row", [(i + stride, i) for i in range(row_devices - stride)])

    def to_ahead(block, stride):
        return lax.ppermute(block, "row", [(i, i + stride) for i in range(row_devices - stride)])

    ahead2 = from_ahead(part, 2)
    joined = pl.pallas_call(
        join_kernel,
        out_shape=jax.ShapeDtypeStruct((2 * NV, part.shape[1]), part.dtype),
        in_specs=[vmem, vmem],
        out_specs=vmem,
        compiler_params=pltpu.CompilerParams(vmem_limit_bytes=28 * 1024 * 1024),
        cost_estimate=estimate(0.5),
        name="joined",
    )(part, ahead2)
    ahead13 = from_ahead(joined, 1)

    meta, a, b, w = pl.pallas_call(
        functools.partial(prepare_kernel, rows_dev),
        out_shape=(
            jax.ShapeDtypeStruct((1, rows_dev * KMAX + 128), jnp.int32),
            jax.ShapeDtypeStruct((cells, FEAT), jnp.bfloat16),
            jax.ShapeDtypeStruct((FEAT, cells), jnp.bfloat16),
            jax.ShapeDtypeStruct((2 * NV, cells), jnp.bfloat16),
        ),
        in_specs=[smem] + [vmem] * 4,
        out_specs=(vmem,) * 4,
        scratch_shapes=[pltpu.VMEM((FEAT, cells), jnp.float32)] * 2,
        compiler_params=pltpu.CompilerParams(vmem_limit_bytes=28 * 1024 * 1024),
        cost_estimate=estimate(4.0),
        name="prepare",
    )(counts, columns.T, coords, sigma, own)

    acc_shape = jax.ShapeDtypeStruct((NV, cells + BLK), jnp.float32)
    half_shape = jax.ShapeDtypeStruct((NV, half_cells), jnp.float32)
    back_shape = jax.ShapeDtypeStruct((NV, half_cells), jnp.bfloat16)
    spare = [
        pltpu.VMEM((NV, half_cells + BLK), jnp.float32),
        pltpu.VMEM((8, half_cells), jnp.float32),
        pltpu.VMEM((FEAT, half_cells), jnp.float32),
        pltpu.VMEM((FEAT, half_cells), jnp.bfloat16),
        pltpu.VMEM((2 * NV, half_cells), jnp.bfloat16),
    ]

    def ahead(phase, tiles, out_shape, scratch, *operands):
        kernel = functools.partial(ahead_kernel, phase, rows_dev)
        return run(kernel, "ahead%d" % phase, tiles, out_shape, spare + scratch, (meta, a, w) + operands)

    acc = run(functools.partial(near_kernel, rows_dev), "near", 16, acc_shape, [], (meta, a, w, b))
    acc, back2 = ahead(2, 75, (acc_shape, back_shape), [], ahead2, acc, b)
    backs_shape = jax.ShapeDtypeStruct((2 * NV, half_cells), jnp.bfloat16)
    acc, backs = ahead(3, 60, (acc_shape, backs_shape), [], ahead13, acc, b, back2)
    got = to_ahead(backs, 2)
    acc_row = [pltpu.VMEM((NV, cells + BLK), jnp.float32)]
    kept, given, back1 = ahead(1, 75, (half_shape, half_shape, half_shape), acc_row, ahead13, acc)
    onward = pl.pallas_call(
        onward_kernel,
        out_shape=back_shape,
        in_specs=[vmem, vmem],
        out_specs=vmem,
        compiler_params=pltpu.CompilerParams(vmem_limit_bytes=28 * 1024 * 1024),
        cost_estimate=estimate(0.5),
        name="onward",
    )(back1, got)
    given, onward = lax.optimization_barrier((given, onward))
    got1 = to_ahead(onward, 1)
    partner = lax.ppermute(given, "col", [(0, 1), (1, 0)])
    inner, scale = run(
        functools.partial(inside_kernel, rows_dev),
        "inside",
        18,
        (half_shape, jax.ShapeDtypeStruct((1, half_cells), jnp.float32)),
        [pltpu.VMEM((NV, half_cells + BLK), jnp.float32)],
        (meta, a, w, b, kept, got, own),
    )
    return (inner + (partner + got1.astype(jnp.float32)) * scale).T


def solution(mesh):
    in_specs = (P(("groups", "row"), None), P(None, "row"), P(("groups", "row")), P(), P())
    out_specs = P(("groups", "row", "col"), None)
    return jax.shard_map(local, mesh=mesh, in_specs=in_specs, out_specs=out_specs, check_vma=False)
```
